128 devices in a mesh: dp: 8 (over y, core), ctx: 16 (over z, x).
Axes of the slice: x: 4, y: 4, z: 4, core: 2. Of those that a mesh axis runs over, the one named last changes fastest.
Arguments:
- query_rows: bfloat16 [32768, 8, 128], P(('dp', 'ctx')), parts along dimension 0, may hold values from -17 to 17
- key_rows: bfloat16 [32768, 128], P(('dp', 'ctx')), parts along dimension 0, may hold values from -17 to 17
- value_rows: bfloat16 [32768, 128], P(('dp', 'ctx')), parts along dimension 0, may hold values from -1.5 to 1.5
- grad_out: bfloat16 [32768, 8, 128], P(('dp', 'ctx')), parts along dimension 0, may hold values from -6 to 6
Outputs:
- attended: bfloat16 [32768, 8, 128], P(('dp', 'ctx')), parts along dimension 0
- grad_query: float32 [32768, 8, 128], P(('dp', 'ctx')), parts along dimension 0
- grad_key: float32 [32768, 128], P(('dp', 'ctx')), parts along dimension 0
- grad_value: float32 [32768, 128], P(('dp', 'ctx')), parts along dimension 0
The draws below stay inside these ranges and needn't reach their ends.
There are 8 independent parts, one for each index of `dp`. The reference program is written for one: setup_inputs(seed, part) draws one part's arguments, and reference() takes and returns one part's arrays. A program takes and returns all parts, laid end to end along the dimension named above; each array names one. Nothing has to cross between parts.
All inputs are finite; a program needn't handle non-finite values.
Results may differ from the reference program's by a relative error of at most 0.022.
Values may be sent and summed in bfloat16 or wider, within the bound.
No kernel may reach another device: no remote copies, remote signals or barrier semaphores. Data moves between devices by JAX's collectives and lax.ppermute only.
A program may use at most 64 MiB of HBM per device.

```python
import jax
import jax.numpy as jnp
from jax import lax

HEADS = 8
HD = 128
BLK = 256
SEQ = 4096
N_CTX = 16


def draw_query_rows(key, part):
    key = jax.random.fold_in(key, 11)
    entries = jax.random.truncated_normal(key, -4.0, 4.0, (SEQ, HEADS, HD), jnp.float32)
    return entries.astype(jnp.bfloat16)


def draw_key_rows(key, part):
    key = jax.random.fold_in(key, 23)
    entries = jax.random.truncated_normal(key, -4.0, 4.0, (SEQ, HD), jnp.float32)
    return entries.astype(jnp.bfloat16)


def levels(stream_key, dims, pieces, least, top_value):
    level, own = 1.0, jax.random.fold_in(stream_key, 6)
    for axis_at, shards_of in pieces:
        draws = jnp.exp(jax.random.uniform(jax.random.fold_in(own, axis_at), (shards_of,), jnp.float32, least / len(pieces), top_value / len(pieces)))
        level = level * jnp.repeat(draws, dims[axis_at] // shards_of).reshape([-1 if axis == axis_at else 1 for axis in range(len(dims))])
    return level


def centred(own_key, shape, deviation, bound, split=(), kind=jnp.bfloat16):
    result = jax.random.normal(own_key, shape, jnp.float32) * deviation
    if len(split) > 0:
        result = levels(own_key, shape, split, -0.22, 0.18) * result
    return jnp.clip(result, min=-bound, max=bound).astype(kind)


def setup_inputs(seed: int = 0, part: int = 0) -> dict:
    streams_of = jax.random.split(jax.random.key(seed), 5)
    part_keys = jax.random.split(jax.random.fold_in(streams_of[4], part), 5)
    query_rows = draw_query_rows(jax.random.fold_in(jax.random.fold_in(streams_of[4], part), 71), part)
    key_rows = draw_key_rows(jax.random.fold_in(jax.random.fold_in(streams_of[4], part), 71), part)
    value_rows = centred(part_keys[2], (SEQ, HD), 0.25, 1.5, ((0, 16),))
    grad_out = centred(part_keys[3], (SEQ, HEADS, HD), 1.0, 6.0, ((0, 16),))
    return dict(query_rows=query_rows, key_rows=key_rows, value_rows=value_rows, grad_out=grad_out)


def reference(query_rows, key_rows, value_rows, grad_out):
    inv_root = HD ** -0.5
    highest = lax.Precision.HIGHEST
    key_float = key_rows.astype(jnp.float32)
    value_float = value_rows.astype(jnp.float32)
    query_blocks = query_rows.reshape(N_CTX, BLK, HEADS, HD)
    grad_blocks = grad_out.reshape(N_CTX, BLK, HEADS, HD)
    col_ids = jnp.arange(SEQ, dtype=jnp.int32)

    def one_block(carried, inputs):
        grad_k, grad_v = carried
        q_block, go_block, block_no = inputs
        q_float = q_block.astype(jnp.float32)
        go_float = go_block.astype(jnp.float32)
        row_ids = block_no * BLK + jnp.arange(BLK, dtype=jnp.int32)
        visible = col_ids[None, :] <= row_ids[:, None]
        scores = jnp.einsum("thd,ud->htu", q_float, key_float, precision=highest) * inv_root
        scores = jnp.where(visible[None], scores, -1.0e30)
        row_max = jnp.max(scores, axis=-1, keepdims=True)
        log_total = row_max + jnp.log(jnp.sum(jnp.exp(scores - row_max), axis=-1, keepdims=True))
        weights = jnp.where(visible[None], jnp.exp(scores - log_total), 0.0)
        weights_b = weights.astype(jnp.bfloat16)
        attended = jnp.einsum("htu,ud->thd", weights, value_float, precision=highest).astype(jnp.bfloat16)
        row_dot = jnp.sum(go_float * attended.astype(jnp.float32), axis=-1).T
        grad_p = jnp.einsum("thd,ud->htu", go_float, value_float, precision=highest)
        grad_s = (weights * (grad_p - row_dot[:, :, None])).astype(jnp.bfloat16)
        grad_s_float = grad_s.astype(jnp.float32)
        grad_q = jnp.einsum("htu,ud->thd", grad_s_float, key_float, precision=highest) * inv_root
        grad_k = grad_k + jnp.einsum("htu,thd->ud", grad_s_float, q_float, precision=highest) * inv_root
        grad_v = grad_v + jnp.einsum("htu,thd->ud", weights_b.astype(jnp.float32), go_float, precision=highest)
        return (grad_k, grad_v), (attended, grad_q)

    start_sums = (jnp.zeros((SEQ, HD), jnp.float32), jnp.zeros((SEQ, HD), jnp.float32))
    sums, blocks = lax.scan(one_block, start_sums, (query_blocks, grad_blocks, jnp.arange(N_CTX, dtype=jnp.int32)))
    attended = blocks[0].reshape(SEQ, HEADS, HD)
    grad_query = blocks[1].reshape(SEQ, HEADS, HD)
    return attended, grad_query, sums[0], sums[1]
```

```python
import functools
import math

import jax
import jax.numpy as jnp
from jax import lax
from jax.experimental import pallas as pl
from jax.experimental.pallas import tpu as pltpu
from jax.sharding import PartitionSpec as P
f32 = jnp.float32
bf = jnp.bfloat16
NEG = -1e30

def mm(a, b, ca, cb):
    return lax.dot_general(a, b, (((ca,), (cb,)), ((), ())), preferred_element_type=f32)

def attend_kernel(tc, heads, idx, q, go, kv, att, dq, dkv, s_all, stat, o_t, dq_t):
    me = idx[0]
    rows, hd = q.shape
    blk = kv.shape[1]
    root = hd ** -0.5
    lg = root * math.log2(math.e)
    n = rows // tc
    cols = [slice(c * tc, (c + 1) * tc) for c in range(n)]
    stat[0:8, :] = jnp.full((8, rows), NEG, f32)

    def put(j, masked):
        k = kv[j, :, :hd]
        for c in cols:
            s = mm(k, q[c, :], 1, 1) * lg
            if masked:
                u = lax.broadcasted_iota(jnp.int32, (blk, tc), 0)
                t = (lax.broadcasted_iota(jnp.int32, (blk, tc), 1) + c.start) // heads
                s = jnp.where(u <= t, s, NEG)
            s_all[j, :, c] = s
            stat[0:8, c] = jnp.maximum(stat[0:8, c], jnp.max(s.reshape(blk // 8, 8, tc), axis=0))

    lax.fori_loop(0, me, lambda j, x: (put(j, False), x)[1], 0)
    put(me, True)
    stat[8:16, :] = jnp.broadcast_to(jnp.max(stat[0:8, :], axis=0, keepdims=True), (8, rows))
    stat[16:24, :] = jnp.zeros((8, rows), f32)
    o_t[...] = jnp.zeros_like(o_t)

    def weigh(j, x):
        v = kv[j, :, hd:]
        for c in cols:
            p = jnp.exp2(s_all[j, :, c] - stat[8:9, c])
            stat[16:24, c] += jnp.sum(p.reshape(blk // 8, 8, tc), axis=0)
            o_t[:, c] += mm(v, p.astype(bf), 0, 0)
        return x

    lax.fori_loop(0, me + 1, weigh, 0)
    for c in cols:
        total = jnp.sum(stat[16:24, c], axis=0, keepdims=True)
        a_t = (o_t[:, c] / total).astype(bf)
        att[c, :] = a_t.T
        dot = jnp.sum(a_t.astype(f32) * go[c, :].T.astype(f32), axis=0, keepdims=True)
        stat[0:1, c] = stat[8:9, c] + jnp.log2(total)
        stat[1:2, c] = dot
    dq_t[...] = jnp.zeros_like(dq_t)

    def back(j, x):
        k = kv[j, :, :hd]
        v = kv[j, :, hd:]
        dk = jnp.zeros((blk, hd), f32)
        dv = jnp.zeros((blk, hd), f32)
        for c in cols:
            w = jnp.exp2(s_all[j, :, c] - stat[0:1, c])
            gp = mm(v, go[c, :], 1, 1)
            gs = (w * (gp - stat[1:2, c])).astype(bf)
            dq_t[:, c] += mm(k, gs, 0, 0)
            dk += mm(gs, q[c, :], 1, 0)
            dv += mm(w.astype(bf), go[c, :], 1, 0)
        dkv[j, :, :hd] = (dk * root).astype(dkv.dtype)
        dkv[j, :, hd:] = dv.astype(dkv.dtype)
        return x

    lax.fori_loop(0, me + 1, back, 0)
    for c in cols:
        dq[c, :] = (dq_t[:, c] * root).T

def attend(idx, q, go, kv, heads, tc=512):
    nb, blk, two = kv.shape
    rows, hd = q.shape
    V = pl.BlockSpec(memory_space=pltpu.VMEM)
    return pl.pallas_call(
        functools.partial(attend_kernel, tc, heads),
        out_shape=(jax.ShapeDtypeStruct((rows, hd), bf), jax.ShapeDtypeStruct((rows, hd), f32), jax.ShapeDtypeStruct((nb, blk, two), bf)),
        in_specs=[pl.BlockSpec(memory_space=pltpu.SMEM), V, V, V],
        out_specs=(V, V, V),
        scratch_shapes=[pltpu.VMEM((nb, blk, rows), f32), pltpu.VMEM((24, rows), f32), pltpu.VMEM((hd, rows), f32), pltpu.VMEM((hd, rows), f32)],
        compiler_params=pltpu.CompilerParams(vmem_limit_bytes=56 * 2**20),
        name="attend",
    )(idx, q, go, kv)


def per_device(query_rows, key_rows, value_rows, grad_out):
    me = lax.axis_index("ctx")
    n = lax.axis_size("ctx")
    blk, heads, hd = query_rows.shape
    q = query_rows.reshape(blk * heads, hd)
    go = grad_out.reshape(blk * heads, hd)
    own = jnp.concatenate([key_rows, value_rows], axis=1)
    kv = lax.all_to_all(jnp.broadcast_to(own[None], (n, blk, 2 * hd)), "ctx", 0, 0)
    idx = me.astype(jnp.int32).reshape(1)
    att, dq, dkv = attend(idx, q, go, kv, heads, 1024)
    parts = lax.all_to_all(dkv, "ctx", 0, 0)
    src = lax.broadcasted_iota(jnp.int32, (n, 1, 1), 0)
    total = jnp.sum(jnp.where(src >= me, parts.astype(f32), 0.0), axis=0)
    return (
        att.reshape(blk, heads, hd),
        dq.reshape(blk, heads, hd),
        total[:, :hd],
        total[:, hd:],
    )


def solution(mesh):
    rows3 = P(("dp", "ctx"), None, None)
    rows2 = P(("dp", "ctx"), None)
    return jax.shard_map(
        per_device,
        mesh=mesh,
        in_specs=(rows3, rows2, rows2, rows3),
        out_specs=(rows3, rows3, rows2, rows2),
        check_vma=False,
    )
```

```python
import functools
import math

import jax
import jax.numpy as jnp
from jax import lax
from jax.experimental import pallas as pl
from jax.experimental.pallas import tpu as pltpu
from jax.sharding import PartitionSpec as P

f32 = jnp.float32
bf = jnp.bfloat16
NEG = -1e30
V = pl.BlockSpec(memory_space=pltpu.VMEM)
S = pl.BlockSpec(memory_space=pltpu.SMEM)
COST = pl.CostEstimate(flops=1000, bytes_accessed=1000, transcendentals=0)
PARAMS = pltpu.CompilerParams(vmem_limit_bytes=26 * 2**20)


def mm(a, b, ca, cb):
    return lax.dot_general(a, b, (((ca,), (cb,)), ((), ())), preferred_element_type=f32)


def sd(shape, dtype):
    return jax.ShapeDtypeStruct(shape, dtype)


def blocks_of(refs):
    found = []
    for ref in refs:
        found += [ref] if len(ref.shape) == 2 else [ref.at[j] for j in range(ref.shape[0])]
    return found


def each(count, diagonal, total, step):
    if diagonal:
        step(0, True)
        for j in range(1, total):
            pl.when(count > j)(functools.partial(step, j, False))
    else:

        @pl.when(count > 0)
        def _():
            for j in range(total):
                step(j, False)


def forward_kernel(heads, n_kv, first, last, cnt, q, go, *refs):
    refs = list(refs)
    kv = blocks_of(refs[:n_kv])
    refs = refs[n_kv:]
    if not first:
        stat_in, o_in = refs[:2]
        refs = refs[2:]
    p_all, stat = refs[:2]
    if last:
        att, final, o_t, s_all = refs[2:]
    else:
        o_t, s_all = refs[2:]
    rows, hd = q.shape
    blk = kv[0].shape[0]
    lg = hd**-0.5 * math.log2(math.e)
    count = cnt[0]
    stat[16:24, :] = jnp.full((8, rows), NEG, f32)

    def put(j, masked):
        s = mm(kv[j][:, :hd], q[...], 1, 1) * lg
        if masked:
            u = lax.broadcasted_iota(jnp.int32, (blk, rows), 0)
            t = lax.broadcasted_iota(jnp.int32, (blk, rows), 1) // heads
            s = jnp.where(u <= t, s, NEG)
        s_all[j] = s
        stat[16:24, :] = jnp.maximum(stat[16:24, :], jnp.max(s.reshape(blk // 8, 8, rows), axis=0))

    each(count, first, len(kv), put)
    top = jnp.max(stat[16:24, :], axis=0, keepdims=True)
    if first:
        o_t[...] = jnp.zeros_like(o_t)
        stat[8:16, :] = jnp.zeros((8, rows), f32)
        stat[0:8, :] = jnp.broadcast_to(top, (8, rows))
    else:
        old = stat_in[0:1, :]
        top = jnp.maximum(old, top)
        shrink = jnp.exp2(old - top)
        stat[0:8, :] = jnp.broadcast_to(top, (8, rows))
        stat[8:16, :] = stat_in[8:16, :] * shrink
        o_t[...] = o_in[...] * shrink

    def weigh(j, masked):
        p = jnp.exp2(s_all[j] - stat[0:1, :])
        stat[8:16, :] += jnp.sum(p.reshape(blk // 8, 8, rows), axis=0)
        p = p.astype(bf)
        p_all[j] = p
        o_t[...] += mm(kv[j][:, hd:], p, 0, 0)

    each(count, first, len(kv), weigh)
    if last:
        total = jnp.sum(stat[8:16, :], axis=0, keepdims=True)
        a_t = (o_t[...] / total).astype(bf)
        att[...] = a_t.T
        dot = jnp.sum(a_t.astype(f32) * go[...].T.astype(f32), axis=0, keepdims=True)
        final[0:8, :] = jnp.broadcast_to(stat[0:1, :] + jnp.log2(total), (8, rows))
        final[8:16, :] = jnp.broadcast_to(dot, (8, rows))


def forward(cnt, q, go, kv, state, last, heads):
    rows, hd = q.shape
    blk = kv[0].shape[-2]
    nb = sum(1 if len(a.shape) == 2 else a.shape[0] for a in kv)
    first = state is None
    outs = [sd((nb, blk, rows), bf), sd((24, rows), f32)]
    outs += [sd((rows, hd), bf), sd((16, rows), f32)] if last else [sd((hd, rows), f32)]
    scratch = [pltpu.VMEM((hd, rows), f32)] if last else []
    return pl.pallas_call(
        functools.partial(forward_kernel, heads, len(kv), first, last),
        out_shape=tuple(outs),
        in_specs=[S] + [V] * (2 + len(kv) + (0 if first else 2)),
        out_specs=(V,) * len(outs),
        scratch_shapes=scratch + [pltpu.VMEM((nb, blk, rows), f32)],
        compiler_params=PARAMS,
        name="forward_last" if last else "forward_first" if first else "forward",
        cost_estimate=COST,
    )(cnt, q, go, *kv, *(state or ()))


def backward_kernel(n_kv, first, last, split, cnt, q, go, p_all, stat, final, *refs):
    refs = list(refs)
    kv = blocks_of(refs[:n_kv])
    refs = refs[n_kv:]
    dq_in = None if first else refs.pop(0)
    if last:
        dq_t = refs.pop()
        dq = refs.pop()
    else:
        dq_t = refs.pop()
    dkv = blocks_of(refs)
    rows, hd = q.shape
    blk = kv[0].shape[0]
    root = hd**-0.5
    dq_t[...] = jnp.zeros_like(dq_t) if first else dq_in[...]
    scale = jnp.exp2(stat[0:1, :] - final[0:1, :])
    dot = final[8:9, :]

    def back(j, masked):
        k = kv[j][:, :hd]
        w = p_all[j].astype(f32) * scale
        gp = mm(kv[j][:, hd:], go[...], 1, 1)
        gs = (w * (gp - dot)).astype(bf)
        dq_t[...] += mm(k, gs, 0, 0)
        dkv[j][:, :hd] = (mm(gs, q[...], 1, 0) * root).astype(bf)
        dkv[j][:, hd:] = mm(w.astype(bf), go[...], 1, 0).astype(bf)

    if last:
        for j in range(1, len(kv)):
            dkv[j][...] = jnp.zeros((blk, 2 * hd), bf)
    each(cnt[0], last, len(kv), back)
    if last:
        dq[...] = (dq_t[...] * root).T


def backward(cnt, q, go, p_all, stat, final, kv, dq_t, last, split):
    rows, hd = q.shape
    nb, blk = p_all.shape[:2]
    first = dq_t is None
    outs = [sd((blk, 2 * hd), bf)] * nb if split else [sd((nb, blk, 2 * hd), bf)]
    outs += [sd((rows, hd), f32) if last else sd((hd, rows), f32)]
    return pl.pallas_call(
        functools.partial(backward_kernel, len(kv), first, last, split),
        out_shape=tuple(outs),
        in_specs=[S] + [V] * (5 + len(kv) + (0 if first else 1)),
        out_specs=(V,) * len(outs),
        scratch_shapes=[pltpu.VMEM((hd, rows), f32)] if last else [],
        compiler_params=PARAMS,
        name="backward_last" if last else "backward",
        cost_estimate=COST,
    )(cnt, q, go, p_all, stat, final, *kv, *([] if first else [dq_t]))


def per_device(query_rows, key_rows, value_rows, grad_out):
    me = lax.axis_index("ctx").astype(jnp.int32)
    n = lax.axis_size("ctx")
    side = math.isqrt(n)
    z, x = me // side, me % side
    blk, heads, hd = query_rows.shape
    q = query_rows.reshape(blk * heads, hd)
    go = grad_out.reshape(blk * heads, hd)

    def along_x(value, by):
        return lax.ppermute(value, "ctx", [(i, i // side * side + (i + by) % side) for i in range(n)])

    def along_z(value, by):
        pairs = [(i, i + side * by) for i in range(n) if 0 <= i + side * by < n]
        return lax.ppermute(value, "ctx", pairs)

    own = jnp.concatenate([key_rows, value_rows], axis=1)
    steps = range(1, side)
    far2 = along_z(own, 2)
    line = jnp.stack([own] + [along_x(own, r) for r in steps])
    far1 = along_z(line, 1)
    far3 = along_z(line, 3)
    far2 = [far2] + [along_x(far2, r) for r in steps]
    count = {r: jnp.where(z >= r, side, 0).astype(jnp.int32).reshape(1) for r in steps}
    count[0] = (x + 1).reshape(1)
    kvs = {0: [line], 1: [far1], 3: [far3], 2: far2}
    p, top = {}, {}
    state = None
    for r in (0, 1, 3):
        p[r], *state = forward(count[r], q, go, kvs[r], state, False, heads)
        top[r] = state[0]
    p[2], top[2], att, final = forward(count[2], q, go, kvs[2], state, True, heads)

    def back(r, dq_t, last, split):
        return backward(count[r], q, go, p[r], top[r], final, kvs[r], dq_t, last, split)

    *part2, dq_t = back(2, None, False, True)
    part2 = [part2[0]] + [along_x(part2[r], -r) for r in steps]
    part3, dq_t = back(3, dq_t, False, False)
    part3 = along_z(part3, -3)
    sum2 = sum(a.astype(f32) for a in part2).astype(bf)
    sum2 = along_z(sum2, -2)
    part1, dq_t = back(1, dq_t, False, False)
    part1 = along_z(part1, -1)
    *part0, dq = back(0, dq_t, True, True)
    total = [part0[r].astype(f32) + part3[r].astype(f32) + part1[r].astype(f32) for r in range(side)]
    grads = total[0] + sum2.astype(f32)
    for r in steps:
        grads += along_x(total[r].astype(bf), -r).astype(f32)
    return (att.reshape(blk, heads, hd), dq.reshape(blk, heads, hd), grads[:, :hd], grads[:, hd:])


def solution(mesh):
    rows3 = P(("dp", "ctx"), None, None)
    rows2 = P(("dp", "ctx"), None)
    return jax.shard_map(
        per_device,
        mesh=mesh,
        in_specs=(rows3, rows2, rows2, rows3),
        out_specs=(rows3, rows3, rows2, rows2),
        check_vma=False,
    )
```

```python
import functools
import math

import jax
import jax.numpy as jnp
from jax import lax
from jax.experimental import pallas as pl
from jax.experimental.pallas import tpu as pltpu
from jax.sharding import PartitionSpec as P

f32 = jnp.float32
bf = jnp.bfloat16
NEG = -1e30
FWD = 1024
MIB = 18
V = pl.BlockSpec(memory_space=pltpu.VMEM)
S = pl.BlockSpec(memory_space=pltpu.SMEM)
COST = pl.CostEstimate(flops=1000, bytes_accessed=1000, transcendentals=0)
PARAMS = pltpu.CompilerParams(vmem_limit_bytes=MIB * 2**20)


def mm(a, b, ca, cb):
    return lax.dot_general(a, b, (((ca,), (cb,)), ((), ())), preferred_element_type=f32)


def sd(shape, dtype):
    return jax.ShapeDtypeStruct(shape, dtype)


def load_kernel(q, go, own, q_out, go_out):
    q_out[...] = q[...]
    go_out[...] = go[...]


def load(q, go, own):
    rows, hd = q.shape
    return pl.pallas_call(
        load_kernel,
        out_shape=(sd((rows, hd), bf), sd((rows, hd), bf)),
        in_specs=[V, V, pl.BlockSpec(memory_space=pl.ANY)],
        out_specs=(V, V),
        compiler_params=PARAMS,
        name="load",
        cost_estimate=COST,
    )(q, go, own)


def blocks_of(refs):
    found = []
    for ref in refs:
        found += [ref] if len(ref.shape) == 2 else [ref.at[j] for j in range(ref.shape[0])]
    return found


def each(count, diagonal, total, step):
    if diagonal:
        step(0, True)
        for j in range(1, total):
            pl.when(count > j)(functools.partial(step, j, False))
    else:

        @pl.when(count > 0)
        def _():
            for j in range(total):
                step(j, False)


def forward_kernel(heads, n_kv, first, last, cnt, q, go, *refs):
    refs = list(refs)
    kv = blocks_of(refs[:n_kv])
    refs = refs[n_kv:]
    if not first:
        stat_in, o_in = refs[:2]
        refs = refs[2:]
    p_all, stat = refs[:2]
    if last:
        att, final, o_t, s_all = refs[2:]
    else:
        o_t, s_all = refs[2:]
    rows, hd = q.shape
    blk = kv[0].shape[0]
    lg = hd**-0.5 * math.log2(math.e)
    count = cnt[0]
    width = min(FWD, rows)

    def put(c, j, masked):
        s = mm(kv[j][:, :hd], q[c, :], 1, 1) * lg
        if masked:
            u = lax.broadcasted_iota(jnp.int32, (blk, width), 0)
            t = (lax.broadcasted_iota(jnp.int32, (blk, width), 1) + c.start) // heads
            s = jnp.where(u <= t, s, NEG)
        s_all[j, :, c] = s
        return jnp.max(s.reshape(blk // 8, 8, width), axis=0)

    def weigh(c, j, top, total, out):
        p = jnp.exp2(s_all[j, :, c].reshape(blk // 8, 8, width) - top[None])
        total = total + jnp.sum(p, axis=0)
        p = p.reshape(blk, width).astype(bf)
        p_all[j, :, c] = p
        return total, out + mm(kv[j][:, hd:], p, 0, 0)

    def chunk(c, js):
        tops = [put(c, j, first and j == 0) for j in js]
        top = jnp.max(functools.reduce(jnp.maximum, tops), axis=0, keepdims=True)
        top = jnp.broadcast_to(top, (8, width))
        if not first:
            old = stat_in[0:8, c]
            top = jnp.maximum(old, top)
        total = jnp.zeros((8, width), f32)
        out = jnp.zeros((hd, width), f32)
        for j in js:
            total, out = weigh(c, j, top, total, out)
        if not first:
            shrink = jnp.exp2(old - top)
            total = total + stat_in[8:16, c] * shrink
            out = out + (o_in[:, c].reshape(hd // 8, 8, width) * shrink[None]).reshape(hd, width)
        stat[0:8, c] = top
        stat[8:16, c] = total
        o_t[:, c] = out

    def finish(c):
        total = jnp.sum(stat[8:16, c], axis=0, keepdims=True)
        share = jnp.broadcast_to(1.0 / total, (8, width))
        a_t = (o_t[:, c].reshape(hd // 8, 8, width) * share[None]).reshape(hd, width).astype(bf)
        att[c, :] = a_t.T
        dot = jnp.sum(a_t.astype(f32) * go[c, :].T.astype(f32), axis=0, keepdims=True)
        final[0:8, c] = stat[0:8, c] + jnp.broadcast_to(jnp.log2(total), (8, width))
        final[8:16, c] = jnp.broadcast_to(dot, (8, width))


    def over(step):
        @pl.loop(0, rows // width)
        def _(i):
            step(pl.ds(pl.multiple_of(i * width, width), width))

    if first:
        for m in range(1, len(kv) + 1):

            @pl.when(count == m)
            def _(m=m):
                over(lambda c: chunk(c, range(m)))
    else:

        @pl.when(count > 0)
        def _():
            over(lambda c: chunk(c, range(len(kv))))

        @pl.when(count == 0)
        def _():
            stat[...] = stat_in[...]
            o_t[...] = o_in[...]

    if last:
        over(finish)


def forward(cnt, q, go, kv, state, last, heads):
    rows, hd = q.shape
    blk = kv[0].shape[-2]
    nb = sum(1 if len(a.shape) == 2 else a.shape[0] for a in kv)
    first = state is None
    outs = [sd((nb, blk, rows), bf), sd((16, rows), f32)]
    outs += [sd((rows, hd), bf), sd((16, rows), f32)] if last else [sd((hd, rows), f32)]
    scratch = [pltpu.VMEM((hd, rows), f32)] if last else []
    return pl.pallas_call(
        functools.partial(forward_kernel, heads, len(kv), first, last),
        out_shape=tuple(outs),
        in_specs=[S] + [V] * (2 + len(kv) + (0 if first else 2)),
        out_specs=(V,) * len(outs),
        scratch_shapes=scratch + [pltpu.VMEM((nb, blk, rows), f32)],
        compiler_params=PARAMS,
        name="forward_last" if last else "forward_first" if first else "forward",
        cost_estimate=COST,
    )(cnt, q, go, *kv, *(state or ()))


def backward_kernel(n_kv, first, last, split, cnt, q, go, p_all, stat, final, *refs):
    refs = list(refs)
    kv = refs[0] if n_kv == 1 else refs[:n_kv]
    refs = refs[n_kv:]
    dq_in = None if first else refs.pop(0)
    nb, blk, rows = p_all.shape
    outs = [refs.pop(0) for _ in range(nb if split else 1)]
    dq = refs.pop(0)
    dq_t = refs.pop(0) if last else dq
    scale = refs.pop(0)
    dkv = refs.pop(0) if split else outs[0]
    hd = q.shape[1]
    root = hd**-0.5

    def block(j):
        return kv[j] if n_kv > 1 else kv.at[j]

    def piece(j):
        w = p_all[j].astype(f32).reshape(blk // 8, 8, rows) * scale[...][None]
        gp = mm(block(j)[:, hd:], go[...], 1, 1).reshape(blk // 8, 8, rows)
        gs = (w * (gp - final[8:16, :][None])).reshape(blk, rows).astype(bf)
        w = w.reshape(blk, rows).astype(bf)
        return mm(gs, q[...], 1, 0), mm(w, go[...], 1, 0), gs

    def back(js):
        found = [piece(j) for j in js]
        for j, (dk, dv, gs) in zip(js, found):
            dkv[j, :, :hd] = (dk * root).astype(bf)
            dkv[j, :, hd:] = dv.astype(bf)
        dq_t[...] += sum(mm(block(j)[:, :hd], gs, 0, 0) for j, (_, _, gs) in zip(js, found))

    dq_t[...] = jnp.zeros_like(dq_t) if first else dq_in[...]

    @pl.when(cnt[0] > 0)
    def _():
        scale[...] = jnp.exp2(stat[0:8, :] - final[0:8, :])

    pl.when(cnt[0] == nb)(functools.partial(back, range(nb)))
    if last:

        @pl.when(cnt[0] < nb)
        def _():
            @pl.loop(0, cnt[0])
            def _(j):
                back([j])

            @pl.loop(cnt[0], nb)
            def _(j):
                dkv[j] = jnp.zeros((blk, 2 * hd), bf)

        dq[...] = (dq_t[...] * root).T
    if split:
        for j in range(nb):
            outs[j][...] = dkv[j]


def backward(cnt, q, go, p_all, stat, final, kv, dq_t, last, split):
    rows, hd = q.shape
    nb, blk = p_all.shape[:2]
    first = dq_t is None
    outs = [sd((blk, 2 * hd), bf)] * nb if split else [sd((nb, blk, 2 * hd), bf)]
    outs += [sd((rows, hd), f32) if last else sd((hd, rows), f32)]
    scratch = [pltpu.VMEM((hd, rows), f32)] if last else []
    scratch += [pltpu.VMEM((8, rows), f32)]
    scratch += [pltpu.VMEM((nb, blk, 2 * hd), bf)] if split else []
    return pl.pallas_call(
        functools.partial(backward_kernel, len(kv), first, last, split),
        out_shape=tuple(outs),
        in_specs=[S] + [V] * (5 + len(kv) + (0 if first else 1)),
        out_specs=(V,) * len(outs),
        scratch_shapes=scratch,
        compiler_params=PARAMS,
        name="backward_last" if last else "backward",
        cost_estimate=COST,
    )(cnt, q, go, p_all, stat, final, *kv, *([] if first else [dq_t]))


def per_device(query_rows, key_rows, value_rows, grad_out):
    me = lax.axis_index("ctx").astype(jnp.int32)
    n = lax.axis_size("ctx")
    side = math.isqrt(n)
    z, x = me // side, me % side
    blk, heads, hd = query_rows.shape
    q = query_rows.reshape(blk * heads, hd)
    go = grad_out.reshape(blk * heads, hd)

    def along_x(value, by):
        return lax.ppermute(value, "ctx", [(i, i // side * side + (i + by) % side) for i in range(n)])

    def along_z(value, by):
        pairs = [(i, i + side * by) for i in range(n) if 0 <= i + side * by < n]
        return lax.ppermute(value, "ctx", pairs)

    own = lax.optimization_barrier(jnp.concatenate([key_rows, value_rows], axis=1))
    q, go = load(q, go, own)
    steps = range(1, side)
    far2 = along_z(own, 2)
    near = [along_x(own, r) for r in steps]
    far2, q, go, *near = lax.optimization_barrier((far2, q, go, *near))
    line = jnp.stack([own] + near)
    far1 = along_z(line, 1)
    far3 = along_z(line, 3)
    far2 = [far2] + [along_x(far2, r) for r in steps]
    count = {r: jnp.where(z >= r, side, 0).astype(jnp.int32).reshape(1) for r in steps}
    count[0] = (x + 1).reshape(1)
    kvs = {0: [line], 1: [far1], 3: [far3], 2: far2}
    p, top = {}, {}
    state = None
    for r in (0, 2, 1):
        p[r], *state = forward(count[r], q, go, kvs[r], state, False, heads)
        top[r] = state[0]
    p[3], top[3], att, final = forward(count[3], q, go, kvs[3], state, True, heads)

    def back(r, dq_t, last, split):
        return backward(count[r], q, go, p[r], top[r], final, kvs[r], dq_t, last, split)

    part1, dq_t = back(1, None, False, False)
    part1 = along_z(part1, -1)
    part3, dq_t = back(3, dq_t, False, False)
    part3 = along_z(part3, -3)
    *part2, dq_t = back(2, dq_t, False, True)
    part2 = [part2[0]] + [along_x(part2[r], -r) for r in steps]
    dq_t, part1 = lax.optimization_barrier((dq_t, part1))
    *part0, dq = back(0, dq_t, True, True)
    part2, part0 = lax.optimization_barrier((part2, part0))
    sum2 = sum(a.astype(f32) for a in part2).astype(bf)
    sum2 = along_z(sum2, -2)
    total = [part0[r].astype(f32) + part3[r].astype(f32) + part1[r].astype(f32) for r in range(side)]
    grads = total[0] + sum2.astype(f32)
    for r in steps:
        grads += along_x(total[r].astype(bf), -r).astype(f32)
    return (att.reshape(blk, heads, hd), dq.reshape(blk, heads, hd), grads[:, :hd], grads[:, hd:])


def solution(mesh):
    rows3 = P(("dp", "ctx"), None, None)
    rows2 = P(("dp", "ctx"), None)
    return jax.shard_map(
        per_device,
        mesh=mesh,
        in_specs=(rows3, rows2, rows2, rows3),
        out_specs=(rows3, rows3, rows2, rows2),
        check_vma=False,
    )
```

```python
import functools
import math

import jax
import jax.numpy as jnp
from jax import lax
from jax.experimental import pallas as pl
from jax.experimental.pallas import tpu as pltpu
from jax.sharding import PartitionSpec as P

f32 = jnp.float32
bf = jnp.bfloat16
NEG = -1e30
FWD = 1024
MIB = 18
V = pl.BlockSpec(memory_space=pltpu.VMEM)
S = pl.BlockSpec(memory_space=pltpu.SMEM)
COST = pl.CostEstimate(flops=1000, bytes_accessed=1000, transcendentals=0)
PARAMS = pltpu.CompilerParams(vmem_limit_bytes=MIB * 2**20)


def mm(a, b, ca, cb):
    return lax.dot_general(a, b, (((ca,), (cb,)), ((), ())), preferred_element_type=f32)


def sd(shape, dtype):
    return jax.ShapeDtypeStruct(shape, dtype)


def load_kernel(q, go, own, q_out, go_out):
    q_out[...] = q[...]
    go_out[...] = go[...]


def load(q, go, own):
    rows, hd = q.shape
    return pl.pallas_call(
        load_kernel,
        out_shape=(sd((rows, hd), bf), sd((rows, hd), bf)),
        in_specs=[V, V, pl.BlockSpec(memory_space=pl.ANY)],
        out_specs=(V, V),
        compiler_params=PARAMS,
        name="load",
        cost_estimate=COST,
    )(q, go, own)


def blocks_of(refs):
    found = []
    for ref in refs:
        found += [ref] if len(ref.shape) == 2 else [ref.at[j] for j in range(ref.shape[0])]
    return found


def each(count, diagonal, total, step):
    if diagonal:
        step(0, True)
        for j in range(1, total):
            pl.when(count > j)(functools.partial(step, j, False))
    else:

        @pl.when(count > 0)
        def _():
            for j in range(total):
                step(j, False)


def forward_kernel(heads, n_kv, first, last, cnt, q, go, *refs):
    refs = list(refs)
    kv = blocks_of(refs[:n_kv])
    refs = refs[n_kv:]
    if not first:
        stat_in, o_in = refs[:2]
        refs = refs[2:]
    p_all, stat = refs[:2]
    if last:
        att, final, o_t, s_all = refs[2:]
    else:
        o_t, s_all = refs[2:]
    rows, hd = q.shape
    blk = kv[0].shape[0]
    lg = hd**-0.5 * math.log2(math.e)
    count = cnt[0]
    width = min(FWD, rows)

    def put(c, j, masked):
        s = mm(kv[j][:, :hd], q[c, :], 1, 1) * lg
        if masked:
            u = lax.broadcasted_iota(jnp.int32, (blk, width), 0)
            t = (lax.broadcasted_iota(jnp.int32, (blk, width), 1) + c.start) // heads
            s = jnp.where(u <= t, s, NEG)
        s_all[j, :, c] = s
        return jnp.max(s.reshape(blk // 8, 8, width), axis=0)

    def weigh(c, j, top, total, out):
        p = jnp.exp2(s_all[j, :, c].reshape(blk // 8, 8, width) - top[None])
        total = total + jnp.sum(p, axis=0)
        p = p.reshape(blk, width).astype(bf)
        p_all[j, :, c] = p
        return total, out + mm(kv[j][:, hd:], p, 0, 0)

    def chunk(c, js):
        tops = [put(c, j, first and j == 0) for j in js]
        top = jnp.max(functools.reduce(jnp.maximum, tops), axis=0, keepdims=True)
        top = jnp.broadcast_to(top, (8, width))
        if not first:
            old = stat_in[0:8, c]
            top = jnp.maximum(old, top)
        total = jnp.zeros((8, width), f32)
        out = jnp.zeros((hd, width), f32)
        for j in js:
            total, out = weigh(c, j, top, total, out)
        if not first:
            shrink = jnp.exp2(old - top)
            total = total + stat_in[8:16, c] * shrink
            out = out + (o_in[:, c].reshape(hd // 8, 8, width) * shrink[None]).reshape(hd, width)
        stat[0:8, c] = top
        stat[8:16, c] = total
        o_t[:, c] = out

    def finish(c):
        total = jnp.sum(stat[8:16, c], axis=0, keepdims=True)
        share = jnp.broadcast_to(1.0 / total, (8, width))
        a_t = (o_t[:, c].reshape(hd // 8, 8, width) * share[None]).reshape(hd, width).astype(bf)
        att[:, c] = a_t
        dot = jnp.sum(a_t.astype(f32) * go[c, :].T.astype(f32), axis=0, keepdims=True)
        final[0:8, c] = stat[0:8, c] + jnp.broadcast_to(jnp.log2(total), (8, width))
        final[8:16, c] = jnp.broadcast_to(dot, (8, width))


    def over(step):
        @pl.loop(0, rows // width)
        def _(i):
            step(pl.ds(pl.multiple_of(i * width, width), width))

    if first:
        for m in range(1, len(kv) + 1):

            @pl.when(count == m)
            def _(m=m):
                over(lambda c: chunk(c, range(m)))
    else:

        @pl.when(count > 0)
        def _():
            over(lambda c: chunk(c, range(len(kv))))

        @pl.when(count == 0)
        def _():
            stat[...] = stat_in[...]
            o_t[...] = o_in[...]

    if last:
        over(finish)


def forward(cnt, q, go, kv, state, last, heads):
    rows, hd = q.shape
    blk = kv[0].shape[-2]
    nb = sum(1 if len(a.shape) == 2 else a.shape[0] for a in kv)
    first = state is None
    outs = [sd((nb, blk, rows), bf), sd((16, rows), f32)]
    outs += [sd((hd, rows), bf), sd((16, rows), f32)] if last else [sd((hd, rows), f32)]
    scratch = [pltpu.VMEM((hd, rows), f32)] if last else []
    return pl.pallas_call(
        functools.partial(forward_kernel, heads, len(kv), first, last),
        out_shape=tuple(outs),
        in_specs=[S] + [V] * (2 + len(kv) + (0 if first else 2)),
        out_specs=(V,) * len(outs),
        scratch_shapes=scratch + [pltpu.VMEM((nb, blk, rows), f32)],
        compiler_params=PARAMS,
        name="forward_last" if last else "forward_first" if first else "forward",
        cost_estimate=COST,
    )(cnt, q, go, *kv, *(state or ()))


def backward_kernel(n_kv, first, last, split, cnt, q, go, p_all, stat, final, *refs):
    refs = list(refs)
    kv = refs[0] if n_kv == 1 else refs[:n_kv]
    refs = refs[n_kv:]
    dq_in = None if first else refs.pop(0)
    nb, blk, rows = p_all.shape
    outs = [refs.pop(0) for _ in range(nb if split else 1)]
    dq_t = refs.pop(0)
    scale = refs.pop(0)
    dkv = refs.pop(0) if split else outs[0]
    hd = q.shape[1]
    root = hd**-0.5

    def block(j):
        return kv[j] if n_kv > 1 else kv.at[j]

    def piece(j):
        w = p_all[j].astype(f32).reshape(blk // 8, 8, rows) * scale[...][None]
        gp = mm(block(j)[:, hd:], go[...], 1, 1).reshape(blk // 8, 8, rows)
        gs = (w * (gp - final[8:16, :][None])).reshape(blk, rows).astype(bf)
        w = w.reshape(blk, rows).astype(bf)
        return mm(gs, q[...], 1, 0), mm(w, go[...], 1, 0), gs

    def back(js):
        found = [piece(j) for j in js]
        for j, (dk, dv, gs) in zip(js, found):
            dkv[j, :, :hd] = (dk * root).astype(bf)
            dkv[j, :, hd:] = dv.astype(bf)
        dq_t[...] += sum(mm(block(j)[:, :hd], gs, 0, 0) for j, (_, _, gs) in zip(js, found))

    dq_t[...] = jnp.zeros_like(dq_t) if first else dq_in[...]

    @pl.when(cnt[0] > 0)
    def _():
        scale[...] = jnp.exp2(stat[0:8, :] - final[0:8, :])

    pl.when(cnt[0] == nb)(functools.partial(back, range(nb)))
    @pl.when(cnt[0] < nb)
    def _():
        if last:
            @pl.loop(0, cnt[0])
            def _(j):
                back([j])

        @pl.loop(cnt[0], nb)
        def _(j):
            dkv[j] = jnp.zeros((blk, 2 * hd), bf)

    if split:
        for j in range(nb):
            outs[j][...] = dkv[j]


def backward(cnt, q, go, p_all, stat, final, kv, dq_t, last, split):
    rows, hd = q.shape
    nb, blk = p_all.shape[:2]
    first = dq_t is None
    outs = [sd((blk, 2 * hd), bf)] * nb if split else [sd((nb, blk, 2 * hd), bf)]
    outs += [sd((hd, rows), f32)]
    scratch = [pltpu.VMEM((8, rows), f32)]
    scratch += [pltpu.VMEM((nb, blk, 2 * hd), bf)] if split else []
    return pl.pallas_call(
        functools.partial(backward_kernel, len(kv), first, last, split),
        out_shape=tuple(outs),
        in_specs=[S] + [V] * (5 + len(kv) + (0 if first else 1)),
        out_specs=(V,) * len(outs),
        scratch_shapes=scratch,
        compiler_params=PARAMS,
        name="backward_last" if last else "backward",
        cost_estimate=COST,
    )(cnt, q, go, p_all, stat, final, *kv, *([] if first else [dq_t]))


def finish_kernel(att_t, dq_t, att, dq):
    att[...] = att_t[...].T
    dq[...] = (dq_t[...] * dq.shape[1] ** -0.5).T


def finish(att_t, dq_t):
    hd, rows = dq_t.shape
    return pl.pallas_call(
        finish_kernel,
        out_shape=(sd((rows, hd), bf), sd((rows, hd), f32)),
        in_specs=[V, V],
        out_specs=(V, V),
        compiler_params=PARAMS,
        name="finish",
        cost_estimate=COST,
    )(att_t, dq_t)


def per_device(query_rows, key_rows, value_rows, grad_out):
    me = lax.axis_index("ctx").astype(jnp.int32)
    n = lax.axis_size("ctx")
    side = math.isqrt(n)
    z, x = me // side, me % side
    blk, heads, hd = query_rows.shape
    q = query_rows.reshape(blk * heads, hd)
    go = grad_out.reshape(blk * heads, hd)

    def along_x(value, by):
        return lax.ppermute(value, "ctx", [(i, i // side * side + (i + by) % side) for i in range(n)])

    def along_z(value, by, wrap=True):
        pairs = [(i, (i + side * by) % n) for i in range(n)]
        if not wrap:
            pairs = [(i, j) for i, j in pairs if (j > i) == (by > 0)]
        return lax.ppermute(value, "ctx", pairs)

    own = lax.optimization_barrier(jnp.concatenate([key_rows, value_rows], axis=1))
    q, go = load(q, go, own)
    steps = range(1, side)
    far2 = along_z(own, 2)
    near = [along_x(own, r) for r in steps]
    far2, q, go, *near = lax.optimization_barrier((far2, q, go, *near))
    line = jnp.stack([own] + near)
    far1 = along_z(line, 1)
    far3 = along_z(line, 3)
    far2 = [far2] + [along_x(far2, r) for r in steps]
    count = {r: jnp.where(z >= r, side, 0).astype(jnp.int32).reshape(1) for r in steps}
    count[0] = (x + 1).reshape(1)
    kvs = {0: [line], 1: [far1], 3: [far3], 2: far2}
    p, top = {}, {}
    state = None
    for r in (0, 2, 1):
        p[r], *state = forward(count[r], q, go, kvs[r], state, False, heads)
        top[r] = state[0]
    p[3], top[3], att, final = forward(count[3], q, go, kvs[3], state, True, heads)

    def back(r, dq_t, last, split):
        return backward(count[r], q, go, p[r], top[r], final, kvs[r], dq_t, last, split)

    part3, dq_t = back(3, None, False, False)
    part3 = along_z(part3, -3, False)
    part1, dq_t = back(1, dq_t, False, False)
    part1 = along_z(part1, -1)
    *part2, dq_t = back(2, dq_t, False, True)
    part2 = [part2[0]] + [along_x(part2[r], -r) for r in steps]
    dq_t, part3 = lax.optimization_barrier((dq_t, part3))
    *part0, dq = back(0, dq_t, True, True)
    part2, part0 = lax.optimization_barrier((part2, part0))
    sum2 = sum(a.astype(f32) for a in part2).astype(bf)
    sum2 = along_z(sum2, -2)
    total = [part0[r].astype(f32) + part3[r].astype(f32) + part1[r].astype(f32) for r in range(side)]
    parts = [along_x(total[r].astype(bf), -r) for r in steps]
    att, dq = finish(att, dq)
    att, dq, sum2, *parts = lax.optimization_barrier((att, dq, sum2, *parts))
    grads = total[0] + sum2.astype(f32)
    for part in parts:
        grads += part.astype(f32)
    return (att.reshape(blk, heads, hd), dq.reshape(blk, heads, hd), grads[:, :hd], grads[:, hd:])


def solution(mesh):
    rows3 = P(("dp", "ctx"), None, None)
    rows2 = P(("dp", "ctx"), None)
    return jax.shard_map(
        per_device,
        mesh=mesh,
        in_specs=(rows3, rows2, rows2, rows3),
        out_specs=(rows3, rows3, rows2, rows2),
        check_vma=False,
    )
```

```python
import functools
import math

import jax
import jax.numpy as jnp
from jax import lax
from jax.experimental import pallas as pl
from jax.experimental.pallas import tpu as pltpu
from jax.sharding import PartitionSpec as P

f32 = jnp.float32
bf = jnp.bfloat16
NEG = -1e30
FWD = 1024
MIB = 18
V = pl.BlockSpec(memory_space=pltpu.VMEM)
S = pl.BlockSpec(memory_space=pltpu.SMEM)
COST = pl.CostEstimate(flops=1000, bytes_accessed=1000, transcendentals=0)
PARAMS = pltpu.CompilerParams(vmem_limit_bytes=MIB * 2**20)


def mm(a, b, ca, cb):
    return lax.dot_general(a, b, (((ca,), (cb,)), ((), ())), preferred_element_type=f32)


def sd(shape, dtype):
    return jax.ShapeDtypeStruct(shape, dtype)


def load_kernel(q, go, own, q_out, go_out):
    q_out[...] = q[...]
    go_out[...] = go[...]


def load(q, go, own):
    rows, hd = q.shape
    return pl.pallas_call(
        load_kernel,
        out_shape=(sd((rows, hd), bf), sd((rows, hd), bf)),
        in_specs=[V, V, pl.BlockSpec(memory_space=pl.ANY)],
        out_specs=(V, V),
        compiler_params=PARAMS,
        name="load",
        cost_estimate=COST,
    )(q, go, own)


def blocks_of(refs):
    found = []
    for ref in refs:
        found += [ref] if len(ref.shape) == 2 else [ref.at[j] for j in range(ref.shape[0])]
    return found


def each(count, diagonal, total, step):
    if diagonal:
        step(0, True)
        for j in range(1, total):
            pl.when(count > j)(functools.partial(step, j, False))
    else:

        @pl.when(count > 0)
        def _():
            for j in range(total):
                step(j, False)


def forward_kernel(heads, n_kv, first, last, cnt, q, go, *refs):
    refs = list(refs)
    kv = blocks_of(refs[:n_kv])
    refs = refs[n_kv:]
    if not first:
        stat_in, o_in = refs[:2]
        refs = refs[2:]
    p_all, stat = refs[:2]
    if last:
        att, final, o_t, s_all = refs[2:]
    else:
        o_t, s_all = refs[2:]
    rows, hd = q.shape
    blk = kv[0].shape[0]
    lg = hd**-0.5 * math.log2(math.e)
    count = cnt[0]
    width = min(FWD, rows)

    def put(c, j, masked):
        s = mm(kv[j][:, :hd], q[c, :], 1, 1) * lg
        if masked:
            u = lax.broadcasted_iota(jnp.int32, (blk, width), 0)
            t = (lax.broadcasted_iota(jnp.int32, (blk, width), 1) + c.start) // heads
            s = jnp.where(u <= t, s, NEG)
        s_all[j, :, c] = s
        return jnp.max(s.reshape(blk // 8, 8, width), axis=0)

    def weigh(c, j, top, total, out):
        p = jnp.exp2(s_all[j, :, c].reshape(blk // 8, 8, width) - top[None])
        total = total + jnp.sum(p, axis=0)
        p = p.reshape(blk, width).astype(bf)
        p_all[j, :, c] = p
        return total, out + mm(kv[j][:, hd:], p, 0, 0)

    def chunk(c, js):
        tops = [put(c, j, first and j == 0) for j in js]
        top = jnp.max(functools.reduce(jnp.maximum, tops), axis=0, keepdims=True)
        top = jnp.broadcast_to(top, (8, width))
        if not first:
            old = stat_in[0:8, c]
            top = jnp.maximum(old, top)
        total = jnp.zeros((8, width), f32)
        out = jnp.zeros((hd, width), f32)
        for j in js:
            total, out = weigh(c, j, top, total, out)
        if not first:
            shrink = jnp.exp2(old - top)
            total = total + stat_in[8:16, c] * shrink
            out = out + (o_in[:, c].reshape(hd // 8, 8, width) * shrink[None]).reshape(hd, width)
        stat[0:8, c] = top
        stat[8:16, c] = total
        o_t[:, c] = out

    def finish(c):
        total = jnp.sum(stat[8:16, c], axis=0, keepdims=True)
        share = jnp.broadcast_to(1.0 / total, (8, width))
        a_t = (o_t[:, c].reshape(hd // 8, 8, width) * share[None]).reshape(hd, width).astype(bf)
        att[:, c] = a_t
        dot = jnp.sum(a_t.astype(f32) * go[c, :].T.astype(f32), axis=0, keepdims=True)
        final[0:8, c] = stat[0:8, c] + jnp.broadcast_to(jnp.log2(total), (8, width))
        final[8:16, c] = jnp.broadcast_to(dot, (8, width))


    def over(step):
        @pl.loop(0, rows // width)
        def _(i):
            step(pl.ds(pl.multiple_of(i * width, width), width))

    if first:
        for m in range(1, len(kv) + 1):

            @pl.when(count == m)
            def _(m=m):
                over(lambda c: chunk(c, range(m)))
    else:

        @pl.when(count > 0)
        def _():
            over(lambda c: chunk(c, range(len(kv))))

        @pl.when(count == 0)
        def _():
            stat[...] = stat_in[...]
            o_t[...] = o_in[...]

    if last:
        over(finish)


def forward(cnt, q, go, kv, state, last, heads):
    rows, hd = q.shape
    blk = kv[0].shape[-2]
    nb = sum(1 if len(a.shape) == 2 else a.shape[0] for a in kv)
    first = state is None
    outs = [sd((nb, blk, rows), bf), sd((16, rows), f32)]
    outs += [sd((hd, rows), bf), sd((16, rows), f32)] if last else [sd((hd, rows), f32)]
    scratch = [pltpu.VMEM((hd, rows), f32)] if last else []
    return pl.pallas_call(
        functools.partial(forward_kernel, heads, len(kv), first, last),
        out_shape=tuple(outs),
        in_specs=[S] + [V] * (2 + len(kv) + (0 if first else 2)),
        out_specs=(V,) * len(outs),
        scratch_shapes=scratch + [pltpu.VMEM((nb, blk, rows), f32)],
        compiler_params=PARAMS,
        name="forward_last" if last else "forward_first" if first else "forward",
        cost_estimate=COST,
    )(cnt, q, go, *kv, *(state or ()))


def backward_kernel(n_kv, first, last, split, cnt, q, go, p_all, stat, final, *refs):
    refs = list(refs)
    kv = refs[0] if n_kv == 1 else refs[:n_kv]
    refs = refs[n_kv:]
    dq_in = None if first else refs.pop(0)
    nb, blk, rows = p_all.shape
    outs = [refs.pop(0) for _ in range(nb if split else 1)]
    dq_t = refs.pop(0)
    scale = refs.pop(0)
    dkv = refs.pop(0) if split else outs[0]
    hd = q.shape[1]
    root = hd**-0.5

    def block(j):
        return kv[j] if n_kv > 1 else kv.at[j]

    def piece(j):
        w = p_all[j].astype(f32).reshape(blk // 8, 8, rows) * scale[...][None]
        gp = mm(block(j)[:, hd:], go[...], 1, 1).reshape(blk // 8, 8, rows)
        gs = (w * (gp - final[8:16, :][None])).reshape(blk, rows).astype(bf)
        w = w.reshape(blk, rows).astype(bf)
        return mm(gs, q[...], 1, 0), mm(w, go[...], 1, 0), gs

    def back(js):
        found = [piece(j) for j in js]
        for j, (dk, dv, gs) in zip(js, found):
            dkv[j, :, :hd] = (dk * root).astype(bf)
            dkv[j, :, hd:] = dv.astype(bf)
        dq_t[...] += sum(mm(block(j)[:, :hd], gs, 0, 0) for j, (_, _, gs) in zip(js, found))

    dq_t[...] = jnp.zeros_like(dq_t) if first else dq_in[...]

    @pl.when(cnt[0] > 0)
    def _():
        scale[...] = jnp.exp2(stat[0:8, :] - final[0:8, :])

    pl.when(cnt[0] == nb)(functools.partial(back, range(nb)))
    @pl.when(cnt[0] < nb)
    def _():
        if last:
            @pl.loop(0, cnt[0])
            def _(j):
                back([j])

        @pl.loop(cnt[0], nb)
        def _(j):
            dkv[j] = jnp.zeros((blk, 2 * hd), bf)

    if split:
        for j in range(nb):
            outs[j][...] = dkv[j]


def backward(cnt, q, go, p_all, stat, final, kv, dq_t, last, split):
    rows, hd = q.shape
    nb, blk = p_all.shape[:2]
    first = dq_t is None
    outs = [sd((blk, 2 * hd), bf)] * nb if split else [sd((nb, blk, 2 * hd), bf)]
    outs += [sd((hd, rows), f32)]
    scratch = [pltpu.VMEM((8, rows), f32)]
    scratch += [pltpu.VMEM((nb, blk, 2 * hd), bf)] if split else []
    return pl.pallas_call(
        functools.partial(backward_kernel, len(kv), first, last, split),
        out_shape=tuple(outs),
        in_specs=[S] + [V] * (5 + len(kv) + (0 if first else 1)),
        out_specs=(V,) * len(outs),
        scratch_shapes=scratch,
        compiler_params=PARAMS,
        name="backward_last" if last else "backward",
        cost_estimate=COST,
    )(cnt, q, go, p_all, stat, final, *kv, *([] if first else [dq_t]))


def finish_kernel(att_t, dq_t, att, dq):
    att[...] = att_t[...].T
    dq[...] = (dq_t[...] * dq.shape[1] ** -0.5).T


def finish(att_t, dq_t):
    hd, rows = dq_t.shape
    return pl.pallas_call(
        finish_kernel,
        out_shape=(sd((rows, hd), bf), sd((rows, hd), f32)),
        in_specs=[V, V],
        out_specs=(V, V),
        compiler_params=PARAMS,
        name="finish",
        cost_estimate=COST,
    )(att_t, dq_t)


def per_device(query_rows, key_rows, value_rows, grad_out):
    me = lax.axis_index("ctx").astype(jnp.int32)
    n = lax.axis_size("ctx")
    side = math.isqrt(n)
    z, x = me // side, me % side
    blk, heads, hd = query_rows.shape
    q = query_rows.reshape(blk * heads, hd)
    go = grad_out.reshape(blk * heads, hd)

    def along_x(value, by):
        return lax.ppermute(value, "ctx", [(i, i // side * side + (i + by) % side) for i in range(n)])

    def along_z(value, by, wrap=True):
        pairs = [(i, (i + side * by) % n) for i in range(n)]
        if not wrap:
            pairs = [(i, j) for i, j in pairs if (j > i) == (by > 0)]
        return lax.ppermute(value, "ctx", pairs)

    own = lax.optimization_barrier(jnp.concatenate([key_rows, value_rows], axis=1))
    q, go = load(q, go, own)
    steps = range(1, side)
    far2 = along_z(own, 2)
    near = [along_x(own, r) for r in steps]
    far2, q, go, *near = lax.optimization_barrier((far2, q, go, *near))
    line = jnp.stack([own] + near)
    far1 = along_z(line, 1)
    far3 = along_z(line, 3)
    far2 = [far2] + [along_x(far2, r) for r in steps]
    count = {r: jnp.where(z >= r, side, 0).astype(jnp.int32).reshape(1) for r in steps}
    count[0] = (x + 1).reshape(1)
    kvs = {0: [line], 1: [far1], 3: [far3], 2: far2}
    p, top = {}, {}
    state = None
    for r in (0, 2, 1):
        p[r], *state = forward(count[r], q, go, kvs[r], state, False, heads)
        top[r] = state[0]
    p[3], top[3], att, final = forward(count[3], q, go, kvs[3], state, True, heads)

    def back(r, dq_t, last, split):
        return backward(count[r], q, go, p[r], top[r], final, kvs[r], dq_t, last, split)

    part3, dq_t = back(3, None, False, False)
    part3 = along_z(part3, -3, False)
    part1, dq_t = back(1, dq_t, False, False)
    part1 = along_z(part1, -1)
    *part2, dq_t = back(2, dq_t, False, True)
    part2 = [part2[0]] + [along_x(part2[r], -r) for r in steps]
    dq_t, part3 = lax.optimization_barrier((dq_t, part3))
    *part0, dq = back(0, dq_t, True, True)
    part2, part0 = lax.optimization_barrier((part2, part0))
    sum2 = sum(a.astype(f32) for a in part2).astype(bf)
    sum2 = along_z(sum2, -2, False)
    total = [part0[r].astype(f32) + part3[r].astype(f32) + part1[r].astype(f32) for r in range(side)]
    parts = [along_x(total[r].astype(bf), -r) for r in steps]
    att, dq = finish(att, dq)
    parts, att, dq, sum2 = lax.optimization_barrier((parts, att, dq, sum2))
    grads = total[0] + sum2.astype(f32)
    for part in parts:
        grads += part.astype(f32)
    return (att.reshape(blk, heads, hd), dq.reshape(blk, heads, hd), grads[:, :hd], grads[:, hd:])


def solution(mesh):
    rows3 = P(("dp", "ctx"), None, None)
    rows2 = P(("dp", "ctx"), None)
    return jax.shard_map(
        per_device,
        mesh=mesh,
        in_specs=(rows3, rows2, rows2, rows3),
        out_specs=(rows3, rows3, rows2, rows2),
        check_vma=False,
    )
```

```python
import functools
import math

import jax
import jax.numpy as jnp
from jax import lax
from jax.experimental import pallas as pl
from jax.experimental.pallas import tpu as pltpu
from jax.sharding import PartitionSpec as P

f32 = jnp.float32
bf = jnp.bfloat16
NEG = -1e30
FWD = 1024
MIB = 18
V = pl.BlockSpec(memory_space=pltpu.VMEM)
S = pl.BlockSpec(memory_space=pltpu.SMEM)
COST = pl.CostEstimate(flops=1000, bytes_accessed=1000, transcendentals=0)
PARAMS = pltpu.CompilerParams(vmem_limit_bytes=MIB * 2**20)


def mm(a, b, ca, cb):
    return lax.dot_general(a, b, (((ca,), (cb,)), ((), ())), preferred_element_type=f32)


def sd(shape, dtype):
    return jax.ShapeDtypeStruct(shape, dtype)


def load_kernel(q, go, own, q_out, go_out):
    q_out[...] = q[...]
    go_out[...] = go[...]


def load(q, go, own):
    rows, hd = q.shape
    return pl.pallas_call(
        load_kernel,
        out_shape=(sd((rows, hd), bf), sd((rows, hd), bf)),
        in_specs=[V, V, pl.BlockSpec(memory_space=pl.ANY)],
        out_specs=(V, V),
        compiler_params=PARAMS,
        name="load",
        cost_estimate=COST,
    )(q, go, own)


def blocks_of(refs):
    found = []
    for ref in refs:
        found += [ref] if len(ref.shape) == 2 else [ref.at[j] for j in range(ref.shape[0])]
    return found


def each(count, diagonal, total, step):
    if diagonal:
        step(0, True)
        for j in range(1, total):
            pl.when(count > j)(functools.partial(step, j, False))
    else:

        @pl.when(count > 0)
        def _():
            for j in range(total):
                step(j, False)


def forward_kernel(heads, n_kv, first, last, cnt, q, go, *refs):
    refs = list(refs)
    kv = blocks_of(refs[:n_kv])
    refs = refs[n_kv:]
    if not first:
        stat_in, o_in = refs[:2]
        refs = refs[2:]
    p_all, stat = refs[:2]
    if last:
        att, final, o_t, s_all = refs[2:]
    else:
        o_t, s_all = refs[2:]
    rows, hd = q.shape
    blk = kv[0].shape[0]
    lg = hd**-0.5 * math.log2(math.e)
    count = cnt[0]
    width = min(FWD, rows)

    def put(c, j, masked):
        s = mm(kv[j][:, :hd], q[c, :], 1, 1) * lg
        if masked:
            u = lax.broadcasted_iota(jnp.int32, (blk, width), 0)
            t = (lax.broadcasted_iota(jnp.int32, (blk, width), 1) + c.start) // heads
            s = jnp.where(u <= t, s, NEG)
        s_all[j, :, c] = s
        return jnp.max(s.reshape(blk // 8, 8, width), axis=0)

    def weigh(c, j, top, total, out):
        p = jnp.exp2(s_all[j, :, c].reshape(blk // 8, 8, width) - top[None])
        total = total + jnp.sum(p, axis=0)
        p = p.reshape(blk, width).astype(bf)
        p_all[j, :, c] = p
        return total, out + mm(kv[j][:, hd:], p, 0, 0)

    def chunk(c, js):
        tops = [put(c, j, first and j == 0) for j in js]
        top = jnp.max(functools.reduce(jnp.maximum, tops), axis=0, keepdims=True)
        top = jnp.broadcast_to(top, (8, width))
        if not first:
            old = stat_in[0:8, c]
            top = jnp.maximum(old, top)
        total = jnp.zeros((8, width), f32)
        out = jnp.zeros((hd, width), f32)
        for j in js:
            total, out = weigh(c, j, top, total, out)
        if not first:
            shrink = jnp.exp2(old - top)
            total = total + stat_in[8:16, c] * shrink
            out = out + (o_in[:, c].reshape(hd // 8, 8, width) * shrink[None]).reshape(hd, width)
        stat[0:8, c] = top
        stat[8:16, c] = total
        o_t[:, c] = out

    def finish(c):
        total = jnp.sum(stat[8:16, c], axis=0, keepdims=True)
        share = jnp.broadcast_to(1.0 / total, (8, width))
        a_t = (o_t[:, c].reshape(hd // 8, 8, width) * share[None]).reshape(hd, width).astype(bf)
        att[:, c] = a_t
        dot = jnp.sum(a_t.astype(f32) * go[c, :].T.astype(f32), axis=0, keepdims=True)
        final[0:8, c] = stat[0:8, c] + jnp.broadcast_to(jnp.log2(total), (8, width))
        final[8:16, c] = jnp.broadcast_to(dot, (8, width))


    def over(step):
        @pl.loop(0, rows // width)
        def _(i):
            step(pl.ds(pl.multiple_of(i * width, width), width))

    if first:
        for m in range(1, len(kv) + 1):

            @pl.when(count == m)
            def _(m=m):
                over(lambda c: chunk(c, range(m)))
    else:

        @pl.when(count > 0)
        def _():
            over(lambda c: chunk(c, range(len(kv))))

        @pl.when(count == 0)
        def _():
            stat[...] = stat_in[...]
            o_t[...] = o_in[...]

    if last:
        over(finish)


def forward(cnt, q, go, kv, state, last, heads):
    rows, hd = q.shape
    blk = kv[0].shape[-2]
    nb = sum(1 if len(a.shape) == 2 else a.shape[0] for a in kv)
    first = state is None
    outs = [sd((nb, blk, rows), bf), sd((16, rows), f32)]
    outs += [sd((hd, rows), bf), sd((16, rows), f32)] if last else [sd((hd, rows), f32)]
    scratch = [pltpu.VMEM((hd, rows), f32)] if last else []
    return pl.pallas_call(
        functools.partial(forward_kernel, heads, len(kv), first, last),
        out_shape=tuple(outs),
        in_specs=[S] + [V] * (2 + len(kv) + (0 if first else 2)),
        out_specs=(V,) * len(outs),
        scratch_shapes=scratch + [pltpu.VMEM((nb, blk, rows), f32)],
        compiler_params=PARAMS,
        name="forward_last" if last else "forward_first" if first else "forward",
        cost_estimate=COST,
    )(cnt, q, go, *kv, *(state or ()))


def backward_kernel(n_kv, first, last, split, cnt, q, go, p_all, stat, final, *refs):
    refs = list(refs)
    kv = blocks_of(refs[:n_kv])
    refs = refs[n_kv:]
    dq_in = None if first else refs.pop(0)
    nb, blk, rows = p_all.shape
    dkv = blocks_of([refs.pop(0) for _ in range(nb if split else 1)])
    dq_t, scale = refs
    hd = q.shape[1]
    root = hd**-0.5

    def piece(j):
        w = p_all[j].astype(f32).reshape(blk // 8, 8, rows) * scale[...][None]
        gp = mm(kv[j][:, hd:], go[...], 1, 1).reshape(blk // 8, 8, rows)
        gs = (w * (gp - final[8:16, :][None])).reshape(blk, rows).astype(bf)
        w = w.reshape(blk, rows).astype(bf)
        return mm(gs, q[...], 1, 0), mm(w, go[...], 1, 0), gs

    def back(js):
        found = [piece(j) for j in js]
        for j, (dk, dv, _) in zip(js, found):
            dkv[j][:, :hd] = (dk * root).astype(bf)
            dkv[j][:, hd:] = dv.astype(bf)
        return sum(mm(kv[j][:, :hd], gs, 0, 0) for j, (_, _, gs) in zip(js, found))

    def back_one(j):
        dq_t[...] += back([j])

    @pl.when(cnt[0] > 0)
    def _():
        scale[...] = jnp.exp2(stat[0:8, :] - final[0:8, :])

    @pl.when(cnt[0] == nb)
    def _():
        whole = back(range(nb))
        dq_t[...] = whole if first else dq_in[...] + whole

    @pl.when(cnt[0] < nb)
    def _():
        dq_t[...] = jnp.zeros_like(dq_t) if first else dq_in[...]
        for j in range(nb):
            dkv[j][...] = jnp.zeros((blk, 2 * hd), bf)
        if last:
            for j in range(nb - 1):
                pl.when(cnt[0] > j)(functools.partial(back_one, j))


def backward(cnt, q, go, p_all, stat, final, kv, dq_t, last, split):
    rows, hd = q.shape
    nb, blk = p_all.shape[:2]
    first = dq_t is None
    outs = [sd((blk, 2 * hd), bf)] * nb if split else [sd((nb, blk, 2 * hd), bf)]
    outs += [sd((hd, rows), f32)]
    scratch = [pltpu.VMEM((8, rows), f32)]
    return pl.pallas_call(
        functools.partial(backward_kernel, len(kv), first, last, split),
        out_shape=tuple(outs),
        in_specs=[S] + [V] * (5 + len(kv) + (0 if first else 1)),
        out_specs=(V,) * len(outs),
        scratch_shapes=scratch,
        compiler_params=PARAMS,
        name="backward_last" if last else "backward",
        cost_estimate=COST,
    )(cnt, q, go, p_all, stat, final, *kv, *([] if first else [dq_t]))


def finish_kernel(att_t, dq_t, att, dq):
    att[...] = att_t[...].T
    dq[...] = (dq_t[...] * dq.shape[1] ** -0.5).T


def finish(att_t, dq_t):
    hd, rows = dq_t.shape
    return pl.pallas_call(
        finish_kernel,
        out_shape=(sd((rows, hd), bf), sd((rows, hd), f32)),
        in_specs=[V, V],
        out_specs=(V, V),
        compiler_params=PARAMS,
        name="finish",
        cost_estimate=COST,
    )(att_t, dq_t)


def per_device(query_rows, key_rows, value_rows, grad_out):
    me = lax.axis_index("ctx").astype(jnp.int32)
    n = lax.axis_size("ctx")
    side = math.isqrt(n)
    z, x = me // side, me % side
    blk, heads, hd = query_rows.shape
    q = query_rows.reshape(blk * heads, hd)
    go = grad_out.reshape(blk * heads, hd)

    def along_x(value, by):
        return lax.ppermute(value, "ctx", [(i, i // side * side + (i + by) % side) for i in range(n)])

    def along_z(value, by, wrap=True):
        pairs = [(i, (i + side * by) % n) for i in range(n)]
        if not wrap:
            pairs = [(i, j) for i, j in pairs if (j > i) == (by > 0)]
        return lax.ppermute(value, "ctx", pairs)

    own = lax.optimization_barrier(jnp.concatenate([key_rows, value_rows], axis=1))
    q, go = load(q, go, own)
    steps = range(1, side)
    far2 = along_z(own, 2)
    near = [along_x(own, r) for r in steps]
    far2, q, go, *near = lax.optimization_barrier((far2, q, go, *near))
    line = jnp.stack([own] + near)
    far1 = along_z(line, 1)
    far3 = along_z(line, 3)
    far2 = [far2] + [along_x(far2, r) for r in steps]
    count = {r: jnp.where(z >= r, side, 0).astype(jnp.int32).reshape(1) for r in steps}
    count[0] = (x + 1).reshape(1)
    kvs = {0: [line], 1: [far1], 3: [far3], 2: far2}
    p, top = {}, {}
    state = None
    for r in (0, 2, 1):
        p[r], *state = forward(count[r], q, go, kvs[r], state, False, heads)
        top[r] = state[0]
    p[3], top[3], att, final = forward(count[3], q, go, kvs[3], state, True, heads)

    def back(r, dq_t, last, split):
        return backward(count[r], q, go, p[r], top[r], final, kvs[r], dq_t, last, split)

    part3, dq_t = back(3, None, False, False)
    part3 = along_z(part3, -3, False)
    part1, dq_t = back(1, dq_t, False, False)
    part1 = along_z(part1, -1)
    *part2, dq_t = back(2, dq_t, False, True)
    part2 = [part2[0]] + [along_x(part2[r], -r) for r in steps]
    dq_t, part3 = lax.optimization_barrier((dq_t, part3))
    *part0, dq = back(0, dq_t, True, True)
    part2, part0 = lax.optimization_barrier((part2, part0))
    sum2 = sum(a.astype(f32) for a in part2).astype(bf)
    sum2 = along_z(sum2, -2, False)
    total = [part0[r].astype(f32) + part3[r].astype(f32) + part1[r].astype(f32) for r in range(side)]
    parts = [along_x(total[r].astype(bf), -r) for r in steps]
    att, dq = finish(att, dq)
    parts, att, dq, sum2 = lax.optimization_barrier((parts, att, dq, sum2))
    grads = total[0] + sum2.astype(f32)
    for part in parts:
        grads += part.astype(f32)
    return (att.reshape(blk, heads, hd), dq.reshape(blk, heads, hd), grads[:, :hd], grads[:, hd:])


def solution(mesh):
    rows3 = P(("dp", "ctx"), None, None)
    rows2 = P(("dp", "ctx"), None)
    return jax.shard_map(
        per_device,
        mesh=mesh,
        in_specs=(rows3, rows2, rows2, rows3),
        out_specs=(rows3, rows3, rows2, rows2),
        check_vma=False,
    )
```

```python
import functools
import math

import jax
import jax.numpy as jnp
from jax import lax
from jax.experimental import pallas as pl
from jax.experimental.pallas import tpu as pltpu
from jax.sharding import PartitionSpec as P

f32 = jnp.float32
bf = jnp.bfloat16
NEG = -1e30
FWD = 1024
MIB = 18
V = pl.BlockSpec(memory_space=pltpu.VMEM)
S = pl.BlockSpec(memory_space=pltpu.SMEM)
COST = pl.CostEstimate(flops=1000, bytes_accessed=1000, transcendentals=0)
PARAMS = pltpu.CompilerParams(vmem_limit_bytes=MIB * 2**20)


def mm(a, b, ca, cb):
    return lax.dot_general(a, b, (((ca,), (cb,)), ((), ())), preferred_element_type=f32)


def sd(shape, dtype):
    return jax.ShapeDtypeStruct(shape, dtype)


def load_kernel(q, go, own, q_out, go_out):
    q_out[...] = q[...]
    go_out[...] = go[...]


def load(q, go, own):
    rows, hd = q.shape
    return pl.pallas_call(
        load_kernel,
        out_shape=(sd((rows, hd), bf), sd((rows, hd), bf)),
        in_specs=[V, V, pl.BlockSpec(memory_space=pl.ANY)],
        out_specs=(V, V),
        compiler_params=PARAMS,
        name="load",
        cost_estimate=COST,
    )(q, go, own)


def blocks_of(refs):
    found = []
    for ref in refs:
        found += [ref] if len(ref.shape) == 2 else [ref.at[j] for j in range(ref.shape[0])]
    return found


def each(count, diagonal, total, step):
    if diagonal:
        step(0, True)
        for j in range(1, total):
            pl.when(count > j)(functools.partial(step, j, False))
    else:

        @pl.when(count > 0)
        def _():
            for j in range(total):
                step(j, False)


def forward_kernel(heads, n_kv, first, last, cnt, q, go, *refs):
    refs = list(refs)
    kv = blocks_of(refs[:n_kv])
    refs = refs[n_kv:]
    if not first:
        stat_in, o_in = refs[:2]
        refs = refs[2:]
    p_all, stat = refs[:2]
    if last:
        att, final, o_t, s_all = refs[2:]
    else:
        o_t, s_all = refs[2:]
    rows, hd = q.shape
    blk = kv[0].shape[0]
    lg = hd**-0.5 * math.log2(math.e)
    count = cnt[0]
    width = min(FWD, rows)

    def put(c, j, masked):
        s = mm(kv[j][:, :hd], q[c, :], 1, 1) * lg
        if masked:
            u = lax.broadcasted_iota(jnp.int32, (blk, width), 0)
            t = (lax.broadcasted_iota(jnp.int32, (blk, width), 1) + c.start) // heads
            s = jnp.where(u <= t, s, NEG)
        s_all[j, :, c] = s
        return jnp.max(s.reshape(blk // 8, 8, width), axis=0)

    def weigh(c, j, top, total, out):
        p = jnp.exp2(s_all[j, :, c].reshape(blk // 8, 8, width) - top[None])
        total = total + jnp.sum(p, axis=0)
        p = p.reshape(blk, width).astype(bf)
        p_all[j, :, c] = p
        return total, out + mm(kv[j][:, hd:], p, 0, 0)

    def chunk(c, js):
        tops = [put(c, j, first and j == 0) for j in js]
        top = jnp.max(functools.reduce(jnp.maximum, tops), axis=0, keepdims=True)
        top = jnp.broadcast_to(top, (8, width))
        if not first:
            old = stat_in[0:8, c]
            top = jnp.maximum(old, top)
        total = jnp.zeros((8, width), f32)
        out = jnp.zeros((hd, width), f32)
        for j in js:
            total, out = weigh(c, j, top, total, out)
        if not first:
            shrink = jnp.exp2(old - top)
            total = total + stat_in[8:16, c] * shrink
            out = out + (o_in[:, c].reshape(hd // 8, 8, width) * shrink[None]).reshape(hd, width)
        stat[0:8, c] = top
        stat[8:16, c] = total
        o_t[:, c] = out

    def finish(c):
        total = jnp.sum(stat[8:16, c], axis=0, keepdims=True)
        share = jnp.broadcast_to(1.0 / total, (8, width))
        a_t = (o_t[:, c].reshape(hd // 8, 8, width) * share[None]).reshape(hd, width).astype(bf)
        att[:, c] = a_t
        dot = jnp.sum(a_t.astype(f32) * go[c, :].T.astype(f32), axis=0, keepdims=True)
        final[0:8, c] = stat[0:8, c] + jnp.broadcast_to(jnp.log2(total), (8, width))
        final[8:16, c] = jnp.broadcast_to(dot, (8, width))


    def over(step):
        @pl.loop(0, rows // width)
        def _(i):
            step(pl.ds(pl.multiple_of(i * width, width), width))

    if first:
        for m in range(1, len(kv) + 1):

            @pl.when(count == m)
            def _(m=m):
                over(lambda c: chunk(c, range(m)))
    else:

        @pl.when(count > 0)
        def _():
            over(lambda c: chunk(c, range(len(kv))))

        @pl.when(count == 0)
        def _():
            stat[...] = stat_in[...]
            o_t[...] = o_in[...]

    if last:
        over(finish)


def forward(cnt, q, go, kv, state, last, heads):
    rows, hd = q.shape
    blk = kv[0].shape[-2]
    nb = sum(1 if len(a.shape) == 2 else a.shape[0] for a in kv)
    first = state is None
    outs = [sd((nb, blk, rows), bf), sd((16, rows), f32)]
    outs += [sd((hd, rows), bf), sd((16, rows), f32)] if last else [sd((hd, rows), f32)]
    scratch = [pltpu.VMEM((hd, rows), f32)] if last else []
    return pl.pallas_call(
        functools.partial(forward_kernel, heads, len(kv), first, last),
        out_shape=tuple(outs),
        in_specs=[S] + [V] * (2 + len(kv) + (0 if first else 2)),
        out_specs=(V,) * len(outs),
        scratch_shapes=scratch + [pltpu.VMEM((nb, blk, rows), f32)],
        compiler_params=PARAMS,
        name="forward_last" if last else "forward_first" if first else "forward",
        cost_estimate=COST,
    )(cnt, q, go, *kv, *(state or ()))


def backward_kernel(n_kv, first, last, split, cnt, q, go, p_all, stat, final, *refs):
    refs = list(refs)
    kv = refs[0] if n_kv == 1 else refs[:n_kv]
    refs = refs[n_kv:]
    dq_in = None if first else refs.pop(0)
    nb, blk, rows = p_all.shape
    outs = [refs.pop(0) for _ in range(nb if split else 1)]
    dq_t = refs.pop(0)
    scale = refs.pop(0)
    dkv = refs.pop(0) if split else outs[0]
    hd = q.shape[1]
    root = hd**-0.5

    def block(j):
        return kv[j] if n_kv > 1 else kv.at[j]

    def piece(j):
        w = p_all[j].astype(f32).reshape(blk // 8, 8, rows) * scale[...][None]
        gp = mm(block(j)[:, hd:], go[...], 1, 1).reshape(blk // 8, 8, rows)
        gs = (w * (gp - final[8:16, :][None])).reshape(blk, rows).astype(bf)
        w = w.reshape(blk, rows).astype(bf)
        return mm(gs, q[...], 1, 0), mm(w, go[...], 1, 0), gs

    def back(js):
        found = [piece(j) for j in js]
        for j, (dk, dv, gs) in zip(js, found):
            dkv[j, :, :hd] = (dk * root).astype(bf)
            dkv[j, :, hd:] = dv.astype(bf)
        dq_t[...] += sum(mm(block(j)[:, :hd], gs, 0, 0) for j, (_, _, gs) in zip(js, found))

    dq_t[...] = jnp.zeros_like(dq_t) if first else dq_in[...]

    @pl.when(cnt[0] > 0)
    def _():
        scale[...] = jnp.exp2(stat[0:8, :] - final[0:8, :])

    pl.when(cnt[0] == nb)(functools.partial(back, range(nb)))
    @pl.when(cnt[0] < nb)
    def _():
        if last:
            @pl.loop(0, cnt[0])
            def _(j):
                back([j])

        @pl.loop(cnt[0], nb)
        def _(j):
            dkv[j] = jnp.zeros((blk, 2 * hd), bf)

    if split:
        for j in range(nb):
            outs[j][...] = dkv[j]


def backward(cnt, q, go, p_all, stat, final, kv, dq_t, last, split):
    rows, hd = q.shape
    nb, blk = p_all.shape[:2]
    first = dq_t is None
    outs = [sd((blk, 2 * hd), bf)] * nb if split else [sd((nb, blk, 2 * hd), bf)]
    outs += [sd((hd, rows), f32)]
    scratch = [pltpu.VMEM((8, rows), f32)]
    scratch += [pltpu.VMEM((nb, blk, 2 * hd), bf)] if split else []
    return pl.pallas_call(
        functools.partial(backward_kernel, len(kv), first, last, split),
        out_shape=tuple(outs),
        in_specs=[S] + [V] * (5 + len(kv) + (0 if first else 1)),
        out_specs=(V,) * len(outs),
        scratch_shapes=scratch,
        compiler_params=PARAMS,
        name="backward_last" if last else "backward",
        cost_estimate=COST,
    )(cnt, q, go, p_all, stat, final, *kv, *([] if first else [dq_t]))


def finish_kernel(att_t, dq_t, att, dq):
    att[...] = att_t[...].T
    dq[...] = (dq_t[...] * dq.shape[1] ** -0.5).T


def finish(att_t, dq_t):
    hd, rows = dq_t.shape
    return pl.pallas_call(
        finish_kernel,
        out_shape=(sd((rows, hd), bf), sd((rows, hd), f32)),
        in_specs=[V, V],
        out_specs=(V, V),
        compiler_params=PARAMS,
        name="finish",
        cost_estimate=COST,
    )(att_t, dq_t)


def per_device(query_rows, key_rows, value_rows, grad_out):
    me = lax.axis_index("ctx").astype(jnp.int32)
    n = lax.axis_size("ctx")
    side = math.isqrt(n)
    z, x = me // side, me % side
    blk, heads, hd = query_rows.shape
    q = query_rows.reshape(blk * heads, hd)
    go = grad_out.reshape(blk * heads, hd)

    def along_x(value, by):
        return lax.ppermute(value, "ctx", [(i, i // side * side + (i + by) % side) for i in range(n)])

    def along_z(value, by, wrap=True):
        pairs = [(i, (i + side * by) % n) for i in range(n)]
        if not wrap:
            pairs = [(i, j) for i, j in pairs if (j > i) == (by > 0)]
        return lax.ppermute(value, "ctx", pairs)

    own = lax.optimization_barrier(jnp.concatenate([key_rows, value_rows], axis=1))
    q, go = load(q, go, own)
    steps = range(1, side)
    far2 = along_z(own, 2)
    near = [along_x(own, r) for r in steps]
    far2, q, go, *near = lax.optimization_barrier((far2, q, go, *near))
    line = jnp.stack([own] + near)
    far1 = along_z(line, 1)
    far3 = along_z(line, 3)
    far2 = [far2] + [along_x(far2, r) for r in steps]
    count = {r: jnp.where(z >= r, side, 0).astype(jnp.int32).reshape(1) for r in steps}
    count[0] = (x + 1).reshape(1)
    kvs = {0: [line], 1: [far1], 3: [far3], 2: far2}
    p, top = {}, {}
    state = None
    for r in (0, 2, 3):
        p[r], *state = forward(count[r], q, go, kvs[r], state, False, heads)
        top[r] = state[0]
    p[1], top[1], att, final = forward(count[1], q, go, kvs[1], state, True, heads)

    def back(r, dq_t, last, split):
        return backward(count[r], q, go, p[r], top[r], final, kvs[r], dq_t, last, split)

    part3, dq_t = back(3, None, False, False)
    part3 = along_z(part3, -3, False)
    part1, dq_t = back(1, dq_t, False, False)
    part1 = along_z(part1, -1)
    *part2, dq_t = back(2, dq_t, False, True)
    part2 = [part2[0]] + [along_x(part2[r], -r) for r in steps]
    dq_t, part3 = lax.optimization_barrier((dq_t, part3))
    *part0, dq = back(0, dq_t, True, True)
    part2, part0 = lax.optimization_barrier((part2, part0))
    sum2 = sum(a.astype(f32) for a in part2).astype(bf)
    sum2 = along_z(sum2, -2, False)
    total = [part0[r].astype(f32) + part3[r].astype(f32) + part1[r].astype(f32) for r in range(side)]
    parts = [along_x(total[r].astype(bf), -r) for r in steps]
    att, dq = finish(att, dq)
    parts, att, dq, sum2 = lax.optimization_barrier((parts, att, dq, sum2))
    grads = total[0] + sum2.astype(f32)
    for part in parts:
        grads += part.astype(f32)
    return (att.reshape(blk, heads, hd), dq.reshape(blk, heads, hd), grads[:, :hd], grads[:, hd:])


def solution(mesh):
    rows3 = P(("dp", "ctx"), None, None)
    rows2 = P(("dp", "ctx"), None)
    return jax.shard_map(
        per_device,
        mesh=mesh,
        in_specs=(rows3, rows2, rows2, rows3),
        out_specs=(rows3, rows3, rows2, rows2),
        check_vma=False,
    )
```
